512 devices in a mesh: outer: 32 (over y, z_lo), rep: 16 (over z_hi, x, core).
Axes of the slice: x: 4, y: 4, z: 16 (z_hi: 2, z_lo: 8; z = z_hi * 8 + z_lo), core: 2. Of those that a mesh axis runs over, the one named last changes fastest.
Arguments:
- activations: bfloat16 [16, 6144, 4096], P('rep', 'outer'), may hold values from -6 to 6
- out_grads: bfloat16 [16, 4096, 1024], P('rep', 'outer'), may hold values from -0.25 to 0.25
- error_buffer: float32 [16, 6144, 1024], P('rep', 'outer'), may hold values from -6 to 6
- right_factor: float32 [64, 1024], replicated, may hold values from -0.1875 to 0.1875
Outputs:
- update: bfloat16 [1024, 6144], P('rep')
- new_error: float32 [16, 6144, 1024], P('rep', 'outer')
- new_factor: float32 [64, 1024], replicated
The draws below stay inside these ranges and needn't reach their ends.
All inputs are finite; a program needn't handle non-finite values.
Results may differ from the reference program's by a relative error of at most 0.001.
Values may be sent and summed in bfloat16 or wider, within the bound.
A program may use at most 64 MiB of HBM per device.

```python
import jax
import jax.numpy as jnp
from jax import lax

D = 6144
FFS = 1024
RANK = 64
TOK_DEV = 128
TOK_REP = 4096
N_OUTER = 32
N_REP = 16


def shard_levels(own_key, extent, pieces, smallest, high):
    factor_of, own = 1.0, jax.random.fold_in(own_key, 6)
    for position, shards_of in pieces:
        steps = jnp.exp(jax.random.uniform(jax.random.fold_in(own, position), (shards_of,), jnp.float32, smallest / len(pieces), high / len(pieces)))
        factor_of = factor_of * jnp.repeat(steps, extent[position] // shards_of).reshape([-1 if axis == position else 1 for axis in range(len(extent))])
    return factor_of


def gaussian(stream_key, dims, scale, bound, pieces=(), held_as=jnp.bfloat16):
    values = jax.random.normal(stream_key, dims, jnp.float32) * scale
    if len(pieces) > 0:
        values = shard_levels(stream_key, dims, pieces, -0.22, 0.18) * values
    return jnp.clip(values, min=-bound, max=bound).astype(held_as)


def setup_inputs(seed: int = 0) -> dict:
    key_of = jax.random.split(jax.random.key(seed), 5)
    activations = gaussian(key_of[0], (N_REP, D, TOK_REP), 1.0, 6.0, ((0, 16), (1, 32)))
    out_grads = gaussian(key_of[1], (N_REP, TOK_REP, FFS), ((TOK_DEV * N_OUTER) ** -0.5), 0.25, ((0, 16), (1, 32)))
    error_buffer = gaussian(key_of[2], (N_REP, D, FFS), 0.5, 6.0, ((0, 16), (1, 32)), jnp.float32)
    right_factor = gaussian(key_of[3], (RANK, FFS), FFS ** -0.5, 0.1875, (), jnp.float32)
    return {"activations": activations, "out_grads": out_grads, "error_buffer": error_buffer, "right_factor": right_factor}


def orthonormal(p_raw):
    gram = jnp.dot(p_raw.T, p_raw, precision=lax.Precision.HIGHEST)
    shift = 0.0001 * jnp.trace(gram) / RANK
    gram = gram + shift * jnp.eye(RANK, dtype=gram.dtype)
    lower = jnp.linalg.cholesky(gram)
    return jax.scipy.linalg.solve_triangular(lower, p_raw.T, lower=True).T

def reference(activations, out_grads, error_buffer, right_factor):

    def replica(index):
        total = jnp.dot(activations[index].astype(jnp.float32), out_grads[index].astype(jnp.float32), preferred_element_type=jnp.float32)
        return total + error_buffer[index]
    corrected = lax.map(replica, jnp.arange(N_REP, dtype=jnp.int32))
    p_raw = jnp.einsum('rdf,kf->dk', corrected, right_factor, precision=lax.Precision.HIGHEST) / N_REP
    p_orth = orthonormal(p_raw)
    new_factor = jnp.einsum('rdf,dk->kf', corrected, p_orth, precision=lax.Precision.HIGHEST) / N_REP
    approx = jnp.dot(p_orth, new_factor, precision=lax.Precision.HIGHEST)
    return (approx.T.astype(jnp.bfloat16), corrected - approx[None], new_factor)
```

```python
import functools

import jax
import jax.numpy as jnp
from jax import lax
from jax.experimental import pallas as pl
from jax.experimental.pallas import tpu as pltpu
from jax.sharding import PartitionSpec as P

HI = lax.Precision.HIGHEST
F32 = jnp.float32


def dot(a, b, ca, cb, precision=None):
    return lax.dot_general(
        a, b, (((ca,), (cb,)), ((), ())), precision=precision, preferred_element_type=F32
    )


def copy_to(src, dst, send, recv, outer, rep):
    return pltpu.make_async_remote_copy(
        src_ref=src,
        dst_ref=dst,
        send_sem=send,
        recv_sem=recv,
        device_id={"outer": outer, "rep": rep},
        device_id_type=pl.DeviceIdType.MESH,
    )


class Round:
    def __init__(self, n, me, place, src, dst, send, recv, first):
        self.out, self.into = [], []
        for k in range(1, n):
            to, frm = lax.rem(me + k, n), lax.rem(me + n - k, n)
            s, r = send.at[first + k - 1], recv.at[first + k - 1]
            self.out.append(copy_to(src(to), dst(me), s, r, *place(to)))
            self.into.append(copy_to(src(to), dst(frm), s, r, *place(to)))

    def start(self):
        for c in self.out:
            c.start()

    def wait(self):
        for c in self.into:
            c.wait_recv()

    def drain(self):
        for c in self.out:
            c.wait_send()


def kernel(
    ny, nz, nh, replicas,
    a_ref, g_ref, e_ref, r_ref,
    update_ref, error_ref, factor_ref,
    g_all, corr, p_part, p_rs, p_h, p_all8,
    pt_all, gram_y, gram_z1, gram_z2, gram_all,
    m_part, m_rs, m_y_src, m_y, m_z1, m_z2, m_agy, m_all,
    z_send, z_recv, yp_send, yp_recv, ym_send, ym_recv,
    rp_send, rp_recv, rm_send, rm_recv, send, recv,
):
    ng = replicas // nh
    zq = nz // 2
    blocks = ny * nz
    tok, width = g_ref.shape
    rank = r_ref.shape[0]
    rows = a_ref.shape[0]
    outer, rep = lax.axis_index("outer"), lax.axis_index("rep")
    y, z = outer // nz, outer % nz
    h, g = rep // ng, rep % ng
    core = rep % 2
    zlow, zhalf = z % zq, z // zq
    y_up, y_down, y_far = (y + 1) % ny, (y + ny - 1) % ny, (y + 2) % ny
    h_other = (h + 1) % nh

    barrier = pltpu.get_barrier_semaphore()
    peers = [((y + k) % ny * nz + z, rep) for k in range(1, ny)]
    peers += [(y * nz + (z + k) % nz, rep) for k in range(1, nz)]
    peers += [(outer, h * ng + (g + k) % ng) for k in range(1, ng)]
    peers += [(outer, h_other * ng + g), (y * nz + (z + zq) % nz, h_other * ng + g)]
    for o, r in peers:
        pl.semaphore_signal(
            barrier, inc=1, device_id={"outer": o, "rep": r},
            device_id_type=pl.DeviceIdType.MESH,
        )
    g_all[outer] = g_ref[...]
    corr[...] = e_ref[...]
    pl.semaphore_wait(barrier, len(peers))

    half = tok // 2
    step_n = min(256, width)

    def multiply(block):
        a = a_ref[:, pl.ds(pl.multiple_of(block * tok, tok), tok)]
        for n in range(0, width, step_n):
            corr[:, n : n + step_n] += dot(a, g_all[block, :, n : n + step_n], 1, 0)

    def place_of(q):
        d = (q + 1) // 2
        return z + d * (1 - 2 * (q % 2))

    def z_copy(zb, q, to):
        slot = g_all.at[y * nz + zb]
        return copy_to(slot, slot, z_send.at[q], z_recv.at[q], y * nz + to, rep)

    def yp_copy(yb, zb, q):
        slot = g_all.at[yb * nz + zb]
        return copy_to(slot, slot, yp_send.at[q], yp_recv.at[q], y_up * nz + z, rep)

    def ym_copy(yb, zb, q):
        slot = g_all.at[yb * nz + zb]
        return copy_to(slot, slot, ym_send.at[q], ym_recv.at[q], y_down * nz + z, rep)

    def rp_copy(yb, zb, q):
        slot = g_all.at[yb * nz + zb, pl.ds(0, half)]
        return copy_to(slot, slot, rp_send.at[q], rp_recv.at[q], y_up * nz + z, rep)

    def rm_copy(yb, zb, q):
        slot = g_all.at[yb * nz + zb, pl.ds(half, half)]
        return copy_to(slot, slot, rm_send.at[q], rm_recv.at[q], y_down * nz + z, rep)

    def inside(zb):
        return jnp.logical_and(zb >= 0, zb < nz)

    for q, to in ((1, z + 1), (2, z - 1)):

        @pl.when(inside(to))
        def _():
            z_copy(z, q, to).start()

    yp_copy(y, z, 0).start()
    ym_copy(y, z, 0).start()
    multiply(outer)
    last = 2 * nz - 1

    def z_step(q, carry):
        zb = place_of(q)

        @pl.when(inside(zb))
        def _():
            z_copy(zb, q, (z + 1) % nz).wait_recv()
            to = z + 2 * (q % 2) - 1

            @pl.when(inside(to))
            def _():
                z_copy(zb, q + 2, to).start()

            yp_copy(y, zb, q).start()
            ym_copy(y, zb, q).start()
            multiply(y * nz + zb)

        return carry

    lax.fori_loop(1, last, z_step, 0)

    def y_step(q, carry):
        zb = place_of(q)

        @pl.when(inside(zb))
        def _():
            yp_copy(y_down, zb, q).wait_recv()
            rp_copy(y_down, zb, q).start()
            ym_copy(y_up, zb, q).wait_recv()
            rm_copy(y_up, zb, q).start()
            multiply(y_down * nz + zb)
            multiply(y_up * nz + zb)

        return carry

    lax.fori_loop(0, last, y_step, 0)

    def far_step(q, carry):
        zb = place_of(q)

        @pl.when(inside(zb))
        def _():
            rp_copy(y_far, zb, q).wait_recv()
            rm_copy(y_far, zb, q).wait_recv()
            multiply(y_far * nz + zb)

        return carry

    lax.fori_loop(0, last, far_step, 0)

    rows8 = rows // ng
    part = dot(corr[...], r_ref[...], 1, 1, HI) * (1.0 / replicas)
    p_part[...] = part.reshape(ng, rows8, rank)
    group = lambda j: (outer, h * ng + j)
    count = [0]

    def make(n, me, place, src, dst):
        first = count[0]
        count[0] += n - 1
        return Round(n, me, place, src, dst, send, recv, first)

    rounds = []

    def go(*args):
        r = make(*args)
        rounds.append(r)
        r.start()
        return r

    def total(ref, n):
        s = ref[0]
        for i in range(1, n):
            s = s + ref[i]
        return s

    rnd = go(ng, g, group, lambda j: p_part.at[j], lambda i: p_rs.at[i])
    p_rs[g] = p_part[g]
    rnd.wait()
    p_h[h] = total(p_rs, ng)
    if nh > 1:
        rnd = go(nh, h, lambda j: (outer, j * ng + g), lambda j: p_h.at[h], lambda i: p_h.at[i])
        rnd.wait()
    p_all8[g] = total(p_h, nh)
    rnd = go(ng, g, group, lambda j: p_all8.at[g], lambda i: p_all8.at[i])
    rnd.wait()
    p = p_all8[...].reshape(rows, rank)

    r8 = rank // ng
    pt = p.T
    gram_all[...] = dot(pt, pt, 1, 1, HI).reshape(ng, r8, rank)
    gram_y[y] = gram_all[g]
    in_y = lambda j: (j * nz + z, rep)
    in_z1 = lambda j: (y * nz + zhalf * zq + j, rep)
    gram_1 = go(ny, y, in_y, lambda j: gram_y.at[y], lambda i: gram_y.at[i])

    hr = rank // 2
    slot = y * nz + zlow * 2 + zhalf
    pt_all[core, slot] = jnp.where(core == 0, pt[:hr], pt[hr:])
    pt_1 = go(
        2, zhalf, lambda j: (y * nz + j * zq + zlow, rep),
        lambda j: pt_all.at[core, slot],
        lambda i: pt_all.at[core, y * nz + zlow * 2 + i],
    )

    mine = dot(pt, corr[...], 1, 0, HI)
    m_part[...] = mine.reshape(ng, r8, width)
    m_1 = go(ng, g, group, lambda j: m_part.at[j], lambda i: m_rs.at[i])
    m_rs[g] = m_part[g]

    gram_1.wait()
    gram_z1[zlow] = total(gram_y, ny)
    gram_2 = go(zq, zlow, in_z1, lambda j: gram_z1.at[zlow], lambda i: gram_z1.at[i])
    pt_1.wait()
    pair = lambda i: pt_all.at[core, pl.ds(y * nz + i * 2, 2)]
    pt_2 = go(zq, zlow, in_z1, lambda j: pair(zlow), pair)

    m_1.wait()
    wy = width // ny
    s = total(m_rs, ng)
    for i in range(ny):
        m_y_src[i] = s[:, i * wy : (i + 1) * wy]
    m_2 = go(ny, y, in_y, lambda j: m_y_src.at[j], lambda i: m_y.at[i])
    m_y[y] = m_y_src[y]

    gram_2.wait()
    gram_z2[zhalf] = total(gram_z1, zq)
    gram_3 = go(
        2, zhalf, lambda j: (y * nz + j * zq + zlow, rep),
        lambda j: gram_z2.at[zhalf], lambda i: gram_z2.at[i],
    )
    m_2.wait()
    m_z1[zlow] = total(m_y, ny)
    m_3 = go(zq, zlow, in_z1, lambda j: m_z1.at[zlow], lambda i: m_z1.at[i])
    pt_2.wait()
    column = lambda i: pt_all.at[core, pl.ds(i * nz, nz)]
    pt_3 = go(ny, y, in_y, lambda j: column(y), column)

    gram_3.wait()
    gram_all[g] = total(gram_z2, 2)
    gram_4 = go(ng, g, group, lambda j: gram_all.at[g], lambda i: gram_all.at[i])
    m_3.wait()
    w = h * 2 + zhalf
    m_z2[w] = total(m_z1, zq)
    m_4 = go(
        2 * nh, w, lambda j: (y * nz + j % 2 * zq + zlow, j // 2 * ng + g),
        lambda j: m_z2.at[w], lambda i: m_z2.at[i],
    )

    gram_4.wait()
    gram = gram_all[...].reshape(rank, rank)
    ri = lax.broadcasted_iota(jnp.int32, (rank, rank), 0)
    ci = lax.broadcasted_iota(jnp.int32, (rank, rank), 1)
    eye = (ri == ci).astype(F32)
    gram = gram + (0.0001 / rank) * jnp.sum(gram * eye) * eye
    full = jnp.concatenate([gram, eye], axis=1)
    x = [full[i : i + 8] for i in range(0, rank, 8)]
    sub = lax.broadcasted_iota(jnp.int32, (8, 1), 0)

    def eliminate(x, lo, hi):
        x = list(x)
        for j in range(lo, hi):
            b, i = divmod(j, 8)
            row = x[b][i : i + 1]
            scaled = row / row[:, j : j + 1]
            for k in range(b, len(x)):
                col = x[k][:, j : j + 1]
                if k == b:
                    col = jnp.where(sub > i, col, 0.0)
                x[k] = x[k] - col * scaled
        return x

    third = rank // 3
    x = eliminate(x, 0, third)

    m_4.wait()
    m_agy[y] = total(m_z2, 2 * nh) * (1.0 / replicas)
    m_5 = go(ny, y, in_y, lambda j: m_agy.at[y], lambda i: m_agy.at[i])
    pt_3.wait()
    side = lambda i: pt_all.at[i]
    pt_4 = go(2, core, lambda j: (outer, rep // 2 * 2 + j), lambda j: side(core), side)
    x = eliminate(x, third, 2 * third)
    m_5.wait()
    m_all[g] = jnp.concatenate([m_agy[i] for i in range(ny)], axis=1)
    m_6 = go(ng, g, group, lambda j: m_all.at[g], lambda i: m_all.at[i])
    x = eliminate(x, 2 * third, rank)
    full = jnp.concatenate(x, axis=0)
    pivots = jnp.sum(full[:, :rank] * eye, axis=1, keepdims=True)
    inverse = full[:, rank:] * (1.0 / jnp.sqrt(pivots))
    p_orth = dot(p, inverse, 1, 1, HI)

    m_6.wait()
    factor = dot(inverse, m_all[...].reshape(rank, width), 1, 0, HI)
    factor_ref[...] = factor
    for n in range(0, width, step_n):
        error_ref[:, n : n + step_n] = corr[:, n : n + step_n] - dot(
            p_orth, factor[:, n : n + step_n], 1, 0, HI
        )
    columns = width // replicas
    both = factor_ref[:, pl.ds(pl.multiple_of(rep // 2 * (2 * columns), 2 * columns), 2 * columns)]
    own = jnp.where(core == 0, both[:, :columns], both[:, columns:])
    weights = dot(own, inverse, 0, 0, HI)
    pt_4.wait()

    def spread(i, carry):
        yb, zb = i // (nz // 2), i % (nz // 2) * 2

        def decompressed(zb):
            at = yb * nz + zb % zq * 2 + zb // zq
            block = jnp.concatenate([pt_all[0, at], pt_all[1, at]], axis=0)
            return dot(weights, block, 1, 0, HI)

        two = jnp.concatenate([decompressed(zb), decompressed(zb + 1)], axis=1)
        update_ref[:, pl.ds(pl.multiple_of(i * 2 * rows, 2 * rows), 2 * rows)] = two.astype(
            update_ref.dtype
        )
        return carry

    lax.fori_loop(0, blocks // 2, spread, 0)

    for r in rounds:
        r.drain()

    def drain_step(q, carry):
        zb = place_of(q)

        @pl.when(inside(zb))
        def _():
            yp_copy(y, zb, q).wait_send()
            ym_copy(y, zb, q).wait_send()
            rp_copy(y_down, zb, q).wait_send()
            rm_copy(y_up, zb, q).wait_send()

        return carry

    lax.fori_loop(0, last, drain_step, 0)
    for q, to in ((1, z + 1), (2, z - 1)):

        @pl.when(inside(to))
        def _():
            z_copy(z, q, to).wait_send()

    def z_drain(q, carry):
        to = z + 2 * (q % 2) - 1

        @pl.when(jnp.logical_and(inside(place_of(q)), inside(to)))
        def _():
            z_copy(place_of(q), q + 2, to).wait_send()

        return carry

    lax.fori_loop(1, last, z_drain, 0)


def body(ny, nz, nh, activations, out_grads, error_buffer, right_factor):
    replicas = lax.axis_size("rep")
    ng = replicas // nh
    blocks = ny * nz
    _, rows, depth = activations.shape
    _, tok, width = out_grads.shape
    rank = right_factor.shape[0]
    r8, wy, zq = rank // ng, width // ny, nz // 2
    dma = lambda n: pltpu.SemaphoreType.DMA((n,))
    vm = lambda *s: pltpu.VMEM(s, F32)
    update, new_error, new_factor = pl.pallas_call(
        functools.partial(kernel, ny, nz, nh, replicas),
        out_shape=(
            jax.ShapeDtypeStruct((width // replicas, blocks * rows), jnp.bfloat16),
            jax.ShapeDtypeStruct((rows, width), F32),
            jax.ShapeDtypeStruct((rank, width), F32),
        ),
        in_specs=[pl.BlockSpec(memory_space=pltpu.VMEM)] * 4,
        out_specs=[pl.BlockSpec(memory_space=pltpu.VMEM)] * 3,
        scratch_shapes=[
            pltpu.VMEM((blocks, tok, width), jnp.bfloat16),
            vm(rows, width),
            vm(ng, rows // ng, rank),
            vm(ng, rows // ng, rank),
            vm(nh, rows // ng, rank),
            vm(ng, rows // ng, rank),
            vm(2, blocks, rank // 2, rows),
            vm(ny, r8, rank),
            vm(zq, r8, rank),
            vm(2, r8, rank),
            vm(ng, r8, rank),
            vm(ng, r8, width),
            vm(ng, r8, width),
            vm(ny, r8, wy),
            vm(ny, r8, wy),
            vm(zq, r8, wy),
            vm(2 * nh, r8, wy),
            vm(ny, r8, wy),
            vm(ng, r8, width),
        ]
        + [dma(2 * nz + 2)] * 10
        + [dma(80)] * 2,
        compiler_params=pltpu.CompilerParams(
            collective_id=0, has_side_effects=True, vmem_limit_bytes=40 * 2**20
        ),
    )(activations[0], out_grads[0], error_buffer[0], right_factor)
    return (update, new_error[None], new_factor)


def solution(mesh, ny=4, nh=2):
    nz = mesh.shape["outer"] // ny
    placed = (P("rep", "outer", None), P("rep", "outer", None), P("rep", "outer", None), P())
    return jax.shard_map(
        functools.partial(body, ny, nz, nh),
        mesh=mesh,
        in_specs=placed,
        out_specs=(P("rep", None), P("rep", "outer", None), P()),
        check_vma=False,
    )
```

```python
import functools

import jax
import jax.numpy as jnp
from jax import lax
from jax.experimental import pallas as pl
from jax.experimental.pallas import tpu as pltpu
from jax.sharding import PartitionSpec as P

ZROWS = 0
HI = lax.Precision.HIGHEST
F32 = jnp.float32


def dot(a, b, ca, cb, precision=None):
    return lax.dot_general(
        a, b, (((ca,), (cb,)), ((), ())), precision=precision, preferred_element_type=F32
    )


def copy_to(src, dst, send, recv, outer, rep):
    return pltpu.make_async_remote_copy(
        src_ref=src,
        dst_ref=dst,
        send_sem=send,
        recv_sem=recv,
        device_id={"outer": outer, "rep": rep},
        device_id_type=pl.DeviceIdType.MESH,
    )


def parts(x):
    hi = x.astype(jnp.bfloat16)
    return hi, (x - hi.astype(F32)).astype(jnp.bfloat16)


class Round:
    def __init__(self, n, me, place, src, dst, send, recv, first):
        def out(k):
            to = lax.rem(me + k, n)
            return copy_to(src(to), dst(me), send.at[first + k - 1], recv.at[first + k - 1], *place(to))

        def into(k):
            to, frm = lax.rem(me + k, n), lax.rem(me + n - k, n)
            return copy_to(src(to), dst(frm), send.at[first + k - 1], recv.at[first + k - 1], *place(to))

        self.n, self.out, self.into = n, out, into

    def each(self, act):
        if self.n <= 8:
            for k in range(1, self.n):
                act(k)
        else:
            lax.fori_loop(1, self.n, lambda k, carry: (act(k), carry)[1], 0)

    def start(self):
        self.each(lambda k: self.out(k).start())

    def wait(self):
        self.each(lambda k: self.into(k).wait_recv())

    def drain(self):
        self.each(lambda k: self.out(k).wait_send())


def kernel(
    ny, nz, nh, replicas,
    a_ref, g_ref, e_ref, r_ref,
    update_ref, error_ref, factor_ref,
    g_all, a_in, r_in, corr, p_part, p_rs, p_h, p_all8,
    pt_all, gram_y, gram_z, gram_all,
    m_part, m_rs, m_z1, m_z2, m_all, spread_src, load_sem,
    z_send, z_recv, zf_send, zf_recv, yp_send, yp_recv, ym_send, ym_recv,
    rp_send, rp_recv, rm_send, rm_recv, send, recv,
):
    ng = replicas // nh
    zq = nz // 2
    blocks = ny * nz
    tok, width = g_ref.shape
    rank = r_ref.shape[0]
    rows = a_ref.shape[0]
    outer, rep = lax.axis_index("outer"), lax.axis_index("rep")
    y, z = outer // nz, outer % nz
    h, g = rep // ng, rep % ng
    core = rep % 2
    zlow, zhalf = z % zq, z // zq
    y_up, y_down, y_far = (y + 1) % ny, (y + ny - 1) % ny, (y + 2) % ny
    h_other = (h + 1) % nh

    barrier = pltpu.get_barrier_semaphore()
    unit = g * ny + y
    at_unit = lambda j: (j % ny * nz + z, h * ng + j // ny)
    peers = [at_unit((unit + k) % (ng * ny)) for k in range(1, ng * ny)]
    peers += [(y * nz + (z + k) % nz, rep) for k in range(1, nz)]
    peers += [(outer, h_other * ng + g), (y * nz + (z + zq) % nz, h_other * ng + g)]
    for o, r in peers:
        pl.semaphore_signal(
            barrier, inc=1, device_id={"outer": o, "rep": r},
            device_id_type=pl.DeviceIdType.MESH,
        )
    loads = [
        pltpu.make_async_copy(src, dst, load_sem.at[i])
        for i, (src, dst) in enumerate(
            ((g_ref, g_all.at[outer]), (e_ref, corr), (a_ref, a_in), (r_ref, r_in))
        )
    ]
    for c in loads:
        c.start()
    loads[0].wait()
    pl.semaphore_wait(barrier, len(peers))

    half = tok // 2
    step_n = min(256, width)

    def multiply(block):
        a = a_in[:, pl.ds(pl.multiple_of(block * tok, tok), tok)]
        for n in range(0, width, step_n):
            corr[:, n : n + step_n] += dot(a, g_all[block, :, n : n + step_n], 1, 0)

    def place_of(q):
        d = (q + 1) // 2
        return z + d * (1 - 2 * (q % 2))

    def z_copy(zb, q, to):
        slot = g_all.at[y * nz + zb]
        return copy_to(slot, slot, z_send.at[q], z_recv.at[q], y * nz + to, rep)

    def yp_copy(yb, zb, q):
        slot = g_all.at[yb * nz + zb]
        return copy_to(slot, slot, yp_send.at[q], yp_recv.at[q], y_up * nz + z, rep)

    def ym_copy(yb, zb, q):
        slot = g_all.at[yb * nz + zb]
        return copy_to(slot, slot, ym_send.at[q], ym_recv.at[q], y_down * nz + z, rep)

    relayed = half - ZROWS // 2

    def rp_copy(yb, zb, q, n=relayed):
        slot = g_all.at[yb * nz + zb, pl.ds(0, n)]
        return copy_to(slot, slot, rp_send.at[q], rp_recv.at[q], y_up * nz + z, rep)

    def rm_copy(yb, zb, q, n=relayed):
        slot = g_all.at[yb * nz + zb, pl.ds(n, n)]
        return copy_to(slot, slot, rm_send.at[q], rm_recv.at[q], y_down * nz + z, rep)

    def zf_copy(zb, q, to):
        slot = g_all.at[y_far * nz + zb, pl.ds(tok - ZROWS, ZROWS)]
        return copy_to(slot, slot, zf_send.at[q], zf_recv.at[q], y * nz + to, rep)

    def inside(zb):
        return jnp.logical_and(zb >= 0, zb < nz)

    for q, to in ((1, z + 1), (2, z - 1)):

        @pl.when(inside(to))
        def _():
            z_copy(z, q, to).start()

    yp_copy(y, z, 0).start()
    ym_copy(y, z, 0).start()
    for c in loads[1:]:
        c.wait()
    multiply(outer)
    last = 2 * nz - 1

    def z_step(q, send_y=True):
        zb = place_of(q)

        @pl.when(inside(zb))
        def _():
            z_copy(zb, q, (z + 1) % nz).wait_recv()
            to = z + 2 * (q % 2) - 1

            @pl.when(inside(to))
            def _():
                z_copy(zb, q + 2, to).start()

            if send_y:
                z_sent(q)

    def z_sent(q):
        zb = place_of(q)
        yp_copy(y, zb, q).start()
        ym_copy(y, zb, q).start()
        multiply(y * nz + zb)

    def y_step(q, n):
        zb = place_of(q)
        yp_copy(y_down, zb, q).wait_recv()
        rp_copy(y_down, zb, q, n).start()
        ym_copy(y_up, zb, q).wait_recv()
        rm_copy(y_up, zb, q, n).start()

    def y_multiply(q):
        zb = place_of(q)
        multiply(y_down * nz + zb)
        multiply(y_up * nz + zb)

    def far_step(q, n):
        zb = place_of(q)
        rp_copy(y_far, zb, q, n).wait_recv()
        rm_copy(y_far, zb, q, n).wait_recv()
        multiply(y_far * nz + zb)

    def zf_step(q):
        zb = place_of(q)
        zf_copy(zb, q, (z + 1) % nz).wait_recv()
        to = z + 2 * (q % 2) - 1

        @pl.when(inside(to))
        def _():
            zf_copy(zb, q + 2, to).start()

    def loop(lo, hi, step):
        def guarded(q, carry):
            @pl.when(inside(place_of(q)))
            def _():
                step(q)

            return carry

        lax.fori_loop(lo, hi, guarded, 0)

    if ZROWS:
        loop(1, 3, lambda q: z_step(q, False))
        y_step(0, half)
        loop(1, 3, z_sent)
        y_multiply(0)
        loop(3, last, z_step)
        far_step(0, half)
        for q, to in ((1, z + 1), (2, z - 1)):

            @pl.when(inside(to))
            def _():
                zf_copy(z, q, to).start()

        def both(q):
            y_step(q, relayed)
            zf_step(q)
            y_multiply(q)

        loop(1, last, both)
    else:
        loop(1, last, z_step)
        y_step(0, half)
        y_multiply(0)

        def relay(q):
            y_step(q, relayed)
            y_multiply(q)

        loop(1, last, relay)
        far_step(0, half)
    loop(1, last, lambda q: far_step(q, relayed))

    rows8 = rows // ng
    part = dot(corr[...], r_in[...], 1, 1, HI) * (1.0 / replicas)
    p_part[...] = part.reshape(ng, rows8, rank)
    group = lambda j: (outer, h * ng + j)
    count = [0]

    def make(n, me, place, src, dst):
        first = count[0]
        count[0] += n - 1
        return Round(n, me, place, src, dst, send, recv, first)

    rounds = []

    def go(*args):
        r = make(*args)
        rounds.append(r)
        r.start()
        return r

    def total(ref, n):
        s = ref[0]
        for i in range(1, n):
            s = s + ref[i]
        return s

    rnd = go(ng, g, group, lambda j: p_part.at[j], lambda i: p_rs.at[i])
    p_rs[g] = p_part[g]
    rnd.wait()
    p_h[h] = total(p_rs, ng)
    if nh > 1:
        rnd = go(nh, h, lambda j: (outer, j * ng + g), lambda j: p_h.at[h], lambda i: p_h.at[i])
        rnd.wait()
    p_all8[g] = total(p_h, nh)
    rnd = go(ng, g, group, lambda j: p_all8.at[g], lambda i: p_all8.at[i])
    rnd.wait()
    p = p_all8[...].reshape(rows, rank)

    r8 = rank // ng
    pt = p.T
    gram_all[...] = dot(pt, pt, 1, 1, HI).reshape(ng, r8, rank)
    gram_y[y] = gram_all[g]
    in_y = lambda j: (j * nz + z, rep)
    in_z1 = lambda j: (y * nz + zhalf * zq + j, rep)
    gram_1 = go(ny, y, in_y, lambda j: gram_y.at[y], lambda i: gram_y.at[i])

    hr = rank // 2
    slot = y * nz + zlow * 2 + zhalf
    piece = jnp.where(core == 0, pt[:hr], pt[hr:])
    lanes = 128
    tail = piece[:, lanes:]
    pt_all[core, slot, :hr] = piece[:, :lanes]
    pt_all[core, slot, hr:] = jnp.concatenate([tail[: hr // 2], tail[hr // 2 :]], axis=1)
    pt_1 = go(
        2, zhalf, lambda j: (y * nz + j * zq + zlow, rep),
        lambda j: pt_all.at[core, slot],
        lambda i: pt_all.at[core, y * nz + zlow * 2 + i],
    )

    wy = width // ny
    for i in range(ny):
        chunk = dot(pt, corr[:, i * wy : (i + 1) * wy], 1, 0, HI)
        m_part[:, i] = chunk.reshape(ng, r8, wy)
    m_1 = go(
        ng * ny, unit, at_unit, lambda j: m_part.at[j // ny, j % ny], lambda i: m_rs.at[i]
    )
    m_rs[unit] = m_part[g, y]

    gram_1.wait()
    gram_z[z] = total(gram_y, ny)
    gram_2 = go(
        nz, z, lambda j: (y * nz + j, rep), lambda j: gram_z.at[z], lambda i: gram_z.at[i]
    )
    pt_1.wait()
    pair = lambda i: pt_all.at[core, pl.ds(y * nz + i * 2, 2)]
    pt_2 = go(zq, zlow, in_z1, lambda j: pair(zlow), pair)

    m_1.wait()
    m_z1[zlow] = total(m_rs, ng * ny)
    m_3 = go(zq, zlow, in_z1, lambda j: m_z1.at[zlow], lambda i: m_z1.at[i])

    pt_2.wait()
    column = lambda i: pt_all.at[core, pl.ds(i * nz, nz)]
    pt_3 = go(ny, y, in_y, lambda j: column(y), column)
    gram_2.wait()
    gram_all[g] = total(gram_z, nz)
    gram_4 = go(ng, g, group, lambda j: gram_all.at[g], lambda i: gram_all.at[i])
    m_3.wait()
    w = h * 2 + zhalf
    m_z2[w] = total(m_z1, zq)
    m_4 = go(
        2 * nh, w, lambda j: (y * nz + j % 2 * zq + zlow, j // 2 * ng + g),
        lambda j: m_z2.at[w], lambda i: m_z2.at[i],
    )

    gram_4.wait()
    gram = gram_all[...].reshape(rank, rank)
    ri = lax.broadcasted_iota(jnp.int32, (rank, rank), 0)
    ci = lax.broadcasted_iota(jnp.int32, (rank, rank), 1)
    eye = (ri == ci).astype(F32)
    gram = gram + (0.0001 / rank) * jnp.sum(gram * eye) * eye
    full = jnp.concatenate([gram, eye], axis=1)
    x = [full[i : i + 8] for i in range(0, rank, 8)]
    sub = lax.broadcasted_iota(jnp.int32, (8, 1), 0)

    def eliminate(x, lo, hi):
        x = list(x)
        for j in range(lo, hi):
            b, i = divmod(j, 8)
            row = x[b][i : i + 1]
            scaled = row / row[:, j : j + 1]
            for k in range(b, len(x)):
                col = x[k][:, j : j + 1]
                if k == b:
                    col = jnp.where(sub > i, col, 0.0)
                x[k] = x[k] - col * scaled
        return x

    x = eliminate(x, 0, rank)
    m_4.wait()
    m_all[g, y] = total(m_z2, 2 * nh) * (1.0 / replicas)
    in_all = lambda i: m_all.at[i // ny, i % ny]
    m_6 = go(ng * ny, unit, at_unit, lambda j: m_all.at[g, y], in_all)
    pt_3.wait()
    side = lambda i: pt_all.at[i]
    pt_4 = go(2, core, lambda j: (outer, rep // 2 * 2 + j), lambda j: side(core), side)

    full = jnp.concatenate(x, axis=0)
    pivots = jnp.sum(full[:, :rank] * eye, axis=1, keepdims=True)
    inverse = full[:, rank:] * (1.0 / jnp.sqrt(pivots))
    hi, mid = parts(dot(p, inverse, 1, 1, HI))
    p_orth = jnp.concatenate([hi, hi, mid, mid], axis=1)
    for r in rounds[:-2]:
        r.drain()
    for k in (yp_copy, ym_copy):
        k(y, z, 0).wait_send()
    rp_copy(y_down, z, 0, half).wait_send()
    rm_copy(y_up, z, 0, half).wait_send()

    def drain(q):
        zb = place_of(q)
        yp_copy(y, zb, q).wait_send()
        ym_copy(y, zb, q).wait_send()
        rp_copy(y_down, zb, q).wait_send()
        rm_copy(y_up, zb, q).wait_send()
        to = z + 2 * (q % 2) - 1

        @pl.when(inside(to))
        def _():
            z_copy(zb, q + 2, to).wait_send()
            if ZROWS:
                zf_copy(zb, q + 2, to).wait_send()

    loop(1, last, drain)
    for q, to in ((1, z + 1), (2, z - 1)):

        @pl.when(inside(to))
        def _():
            z_copy(z, q, to).wait_send()
            if ZROWS:
                zf_copy(z, q, to).wait_send()

    pt_4.wait()

    def orthogonal(i, carry):
        yb, zb = i // (nz // 2), i % (nz // 2) * 2

        def block(zb):
            at = yb * nz + zb % zq * 2 + zb // zq
            head = jnp.concatenate([pt_all[0, at, :hr], pt_all[1, at, :hr]], axis=0)
            t0, t1 = pt_all[0, at, hr:], pt_all[1, at, hr:]
            w = rows - lanes
            tail = jnp.concatenate([t0[:, :w], t0[:, w:], t1[:, :w], t1[:, w:]], axis=0)
            return jnp.concatenate([head, tail], axis=1)

        two = jnp.concatenate([block(zb), block(zb + 1)], axis=1)
        hi, mid = parts(dot(inverse, two, 1, 0, HI))
        spread_src[i] = jnp.concatenate([hi, mid, hi, mid], axis=0)
        return carry

    lax.fori_loop(0, blocks // 2, orthogonal, 0, unroll=2)

    m_6.wait()
    for i in range(ny):
        cut = slice(i * wy, (i + 1) * wy)
        factor = dot(inverse, m_all[:, i].reshape(rank, wy), 1, 0, HI)
        factor_ref[:, cut] = factor
        hi, mid = parts(factor)
        factor = jnp.concatenate([hi, mid, hi, mid], axis=0)
        error_ref[:, cut] = corr[:, cut] - dot(p_orth, factor, 1, 0)
    columns = width // replicas
    both = factor_ref[:, pl.ds(pl.multiple_of(rep // 2 * (2 * columns), 2 * columns), 2 * columns)]
    hi, mid = parts(jnp.where(core == 0, both[:, :columns], both[:, columns:]))
    own = jnp.concatenate([hi, hi, mid, mid], axis=0)

    def spread(i, carry):
        update_ref[:, pl.ds(pl.multiple_of(i * 2 * rows, 2 * rows), 2 * rows)] = dot(
            own, spread_src[i], 0, 0
        ).astype(update_ref.dtype)
        return carry

    lax.fori_loop(0, blocks // 2, spread, 0, unroll=4)

    pt_4.drain()
    m_6.drain()


def body(ny, nz, nh, activations, out_grads, error_buffer, right_factor):
    replicas = lax.axis_size("rep")
    ng = replicas // nh
    blocks = ny * nz
    _, rows, depth = activations.shape
    _, tok, width = out_grads.shape
    rank = right_factor.shape[0]
    r8, wy, zq = rank // ng, width // ny, nz // 2
    dma = lambda n: pltpu.SemaphoreType.DMA((n,))
    vm = lambda *s: pltpu.VMEM(s, F32)
    update, new_error, new_factor = pl.pallas_call(
        functools.partial(kernel, ny, nz, nh, replicas),
        out_shape=(
            jax.ShapeDtypeStruct((width // replicas, blocks * rows), jnp.bfloat16),
            jax.ShapeDtypeStruct((rows, width), F32),
            jax.ShapeDtypeStruct((rank, width), F32),
        ),
        in_specs=[pl.BlockSpec(memory_space=pltpu.HBM)] * 4,
        out_specs=[pl.BlockSpec(memory_space=pltpu.VMEM)] * 3,
        scratch_shapes=[
            pltpu.VMEM((blocks, tok, width), jnp.bfloat16),
            pltpu.VMEM((rows, depth), jnp.bfloat16),
            vm(rank, width),
            vm(rows, width),
            vm(ng, rows // ng, rank),
            vm(ng, rows // ng, rank),
            vm(nh, rows // ng, rank),
            vm(ng, rows // ng, rank),
            vm(2, blocks, rank // 2 * rows // 128, 128),
            vm(ny, r8, rank),
            vm(nz, r8, rank),
            vm(ng, r8, rank),
            vm(ng, ny, r8, wy),
            vm(ng * ny, r8, wy),
            vm(zq, r8, wy),
            vm(2 * nh, r8, wy),
            vm(ng, ny, r8, wy),
            pltpu.VMEM((blocks // 2, 4 * rank, 2 * rows), jnp.bfloat16),
            dma(4),
        ]
        + [dma(2 * nz + 2)] * 12
        + [dma(112)] * 2,
        compiler_params=pltpu.CompilerParams(
            collective_id=0, has_side_effects=True, vmem_limit_bytes=63 * 2**20
        ),
    )(activations[0], out_grads[0], error_buffer[0], right_factor)
    return (update, new_error[None], new_factor)


def solution(mesh, ny=4, nh=2):
    nz = mesh.shape["outer"] // ny
    placed = (P("rep", "outer", None), P("rep", "outer", None), P("rep", "outer", None), P())
    return jax.shard_map(
        functools.partial(body, ny, nz, nh),
        mesh=mesh,
        in_specs=placed,
        out_specs=(P("rep", None), P("rep", "outer", None), P()),
        check_vma=False,
    )
```

```python
import functools

import jax
import jax.numpy as jnp
from jax import lax
from jax.experimental import pallas as pl
from jax.experimental.pallas import tpu as pltpu
from jax.sharding import PartitionSpec as P

ZROWS = 32
HI = lax.Precision.HIGHEST
F32 = jnp.float32


def dot(a, b, ca, cb, precision=None):
    return lax.dot_general(
        a, b, (((ca,), (cb,)), ((), ())), precision=precision, preferred_element_type=F32
    )


def copy_to(src, dst, send, recv, outer, rep):
    return pltpu.make_async_remote_copy(
        src_ref=src,
        dst_ref=dst,
        send_sem=send,
        recv_sem=recv,
        device_id={"outer": outer, "rep": rep},
        device_id_type=pl.DeviceIdType.MESH,
    )


def parts(x):
    hi = x.astype(jnp.bfloat16)
    return hi, (x - hi.astype(F32)).astype(jnp.bfloat16)


class Round:
    def __init__(self, n, me, place, src, dst, send, recv, first):
        def out(k):
            to = lax.rem(me + k, n)
            return copy_to(src(to), dst(me), send.at[first + k - 1], recv.at[first + k - 1], *place(to))

        def into(k):
            to, frm = lax.rem(me + k, n), lax.rem(me + n - k, n)
            return copy_to(src(to), dst(frm), send.at[first + k - 1], recv.at[first + k - 1], *place(to))

        self.n, self.out, self.into = n, out, into

    def each(self, act):
        if self.n <= 8:
            for k in range(1, self.n):
                act(k)
        else:
            lax.fori_loop(1, self.n, lambda k, carry: (act(k), carry)[1], 0)

    def start(self):
        self.each(lambda k: self.out(k).start())

    def wait(self):
        self.each(lambda k: self.into(k).wait_recv())

    def drain(self):
        self.each(lambda k: self.out(k).wait_send())


def kernel(
    ny, nz, nh, replicas,
    a_ref, g_ref, e_ref, r_ref,
    update_ref, error_ref, factor_ref,
    g_all, a_in, r_in, corr, p_part, p_rs, p_h, p_all8,
    pt_all, gram_y, gram_z, gram_all,
    m_part, m_rs, m_z1, m_z2, m_all, spread_src, load_sem,
    z_send, z_recv, zf_send, zf_recv, yp_send, yp_recv, ym_send, ym_recv,
    rp_send, rp_recv, rm_send, rm_recv, send, recv,
):
    ng = replicas // nh
    zq = nz // 2
    blocks = ny * nz
    tok, width = g_ref.shape
    rank = r_ref.shape[0]
    rows = a_ref.shape[0]
    outer, rep = lax.axis_index("outer"), lax.axis_index("rep")
    y, z = outer // nz, outer % nz
    h, g = rep // ng, rep % ng
    core = rep % 2
    zlow, zhalf = z % zq, z // zq
    y_up, y_down, y_far = (y + 1) % ny, (y + ny - 1) % ny, (y + 2) % ny
    h_other = (h + 1) % nh

    barrier = pltpu.get_barrier_semaphore()
    unit = g * ny + y
    at_unit = lambda j: (j % ny * nz + z, h * ng + j // ny)
    peers = [at_unit((unit + k) % (ng * ny)) for k in range(1, ng * ny)]
    peers += [(y * nz + (z + k) % nz, rep) for k in range(1, nz)]
    peers += [(outer, h_other * ng + g), (y * nz + (z + zq) % nz, h_other * ng + g)]
    for o, r in peers:
        pl.semaphore_signal(
            barrier, inc=1, device_id={"outer": o, "rep": r},
            device_id_type=pl.DeviceIdType.MESH,
        )
    loads = [
        pltpu.make_async_copy(src, dst, load_sem.at[i])
        for i, (src, dst) in enumerate(
            ((g_ref, g_all.at[outer]), (e_ref, corr), (a_ref, a_in), (r_ref, r_in))
        )
    ]
    for c in loads:
        c.start()
    loads[0].wait()
    pl.semaphore_wait(barrier, len(peers))

    half = tok // 2
    step_n = min(256, width)

    def multiply(block):
        a = a_in[:, pl.ds(pl.multiple_of(block * tok, tok), tok)]
        for n in range(0, width, step_n):
            corr[:, n : n + step_n] += dot(a, g_all[block, :, n : n + step_n], 1, 0)

    def place_of(q):
        d = (q + 1) // 2
        return z + d * (1 - 2 * (q % 2))

    def z_copy(zb, q, to):
        slot = g_all.at[y * nz + zb]
        return copy_to(slot, slot, z_send.at[q], z_recv.at[q], y * nz + to, rep)

    def yp_copy(yb, zb, q):
        slot = g_all.at[yb * nz + zb]
        return copy_to(slot, slot, yp_send.at[q], yp_recv.at[q], y_up * nz + z, rep)

    def ym_copy(yb, zb, q):
        slot = g_all.at[yb * nz + zb]
        return copy_to(slot, slot, ym_send.at[q], ym_recv.at[q], y_down * nz + z, rep)

    relayed = half - ZROWS // 2

    def rp_copy(yb, zb, q, n=relayed):
        slot = g_all.at[yb * nz + zb, pl.ds(0, n)]
        return copy_to(slot, slot, rp_send.at[q], rp_recv.at[q], y_up * nz + z, rep)

    def rm_copy(yb, zb, q, n=relayed):
        slot = g_all.at[yb * nz + zb, pl.ds(n, n)]
        return copy_to(slot, slot, rm_send.at[q], rm_recv.at[q], y_down * nz + z, rep)

    def zf_copy(zb, q, to):
        slot = g_all.at[y_far * nz + zb, pl.ds(tok - ZROWS, ZROWS)]
        return copy_to(slot, slot, zf_send.at[q], zf_recv.at[q], y * nz + to, rep)

    def inside(zb):
        return jnp.logical_and(zb >= 0, zb < nz)

    for q, to in ((1, z + 1), (2, z - 1)):

        @pl.when(inside(to))
        def _():
            z_copy(z, q, to).start()

    yp_copy(y, z, 0).start()
    ym_copy(y, z, 0).start()
    for c in loads[1:]:
        c.wait()
    multiply(outer)
    last = 2 * nz - 1

    def z_step(q, send_y=True):
        zb = place_of(q)

        @pl.when(inside(zb))
        def _():
            z_copy(zb, q, (z + 1) % nz).wait_recv()
            to = z + 2 * (q % 2) - 1

            @pl.when(inside(to))
            def _():
                z_copy(zb, q + 2, to).start()

            if send_y:
                z_sent(q)

    def z_sent(q):
        zb = place_of(q)
        yp_copy(y, zb, q).start()
        ym_copy(y, zb, q).start()
        multiply(y * nz + zb)

    def y_step(q, n):
        zb = place_of(q)
        yp_copy(y_down, zb, q).wait_recv()
        rp_copy(y_down, zb, q, n).start()
        ym_copy(y_up, zb, q).wait_recv()
        rm_copy(y_up, zb, q, n).start()

    def y_multiply(q):
        zb = place_of(q)
        multiply(y_down * nz + zb)
        multiply(y_up * nz + zb)

    def far_step(q, n):
        zb = place_of(q)
        rp_copy(y_far, zb, q, n).wait_recv()
        rm_copy(y_far, zb, q, n).wait_recv()
        multiply(y_far * nz + zb)

    def zf_step(q):
        zb = place_of(q)
        zf_copy(zb, q, (z + 1) % nz).wait_recv()
        to = z + 2 * (q % 2) - 1

        @pl.when(inside(to))
        def _():
            zf_copy(zb, q + 2, to).start()

    def loop(lo, hi, step):
        def guarded(q, carry):
            @pl.when(inside(place_of(q)))
            def _():
                step(q)

            return carry

        lax.fori_loop(lo, hi, guarded, 0)

    if ZROWS:
        loop(1, 3, z_step)
        y_step(0, half)
        y_multiply(0)
        loop(3, last, z_step)
        far_step(0, half)
        for q, to in ((1, z + 1), (2, z - 1)):

            @pl.when(inside(to))
            def _():
                zf_copy(z, q, to).start()

        def both(q):
            y_step(q, relayed)
            y_multiply(q)
            zf_step(q)

        loop(1, last, both)
    else:
        loop(1, last, z_step)
        y_step(0, half)
        y_multiply(0)

        def relay(q):
            y_step(q, relayed)
            y_multiply(q)

        loop(1, last, relay)
        far_step(0, half)
    loop(1, last, lambda q: far_step(q, relayed))

    rows8 = rows // ng
    part = dot(corr[...], r_in[...], 1, 1, HI) * (1.0 / replicas)
    p_part[...] = part.reshape(ng, rows8, rank)
    group = lambda j: (outer, h * ng + j)
    count = [0]

    def make(n, me, place, src, dst):
        first = count[0]
        count[0] += n - 1
        return Round(n, me, place, src, dst, send, recv, first)

    rounds = []

    def go(*args):
        r = make(*args)
        rounds.append(r)
        r.start()
        return r

    def total(ref, n):
        s = ref[0]
        for i in range(1, n):
            s = s + ref[i]
        return s

    rnd = go(ng, g, group, lambda j: p_part.at[j], lambda i: p_rs.at[i])
    p_rs[g] = p_part[g]
    rnd.wait()
    p_h[h] = total(p_rs, ng)
    if nh > 1:
        rnd = go(nh, h, lambda j: (outer, j * ng + g), lambda j: p_h.at[h], lambda i: p_h.at[i])
        rnd.wait()
    p_all8[g] = total(p_h, nh)
    rnd = go(ng, g, group, lambda j: p_all8.at[g], lambda i: p_all8.at[i])
    rnd.wait()
    p = p_all8[...].reshape(rows, rank)

    r8 = rank // ng
    pt = p.T
    gram_all[...] = dot(pt, pt, 1, 1, HI).reshape(ng, r8, rank)
    gram_y[y] = gram_all[g]
    in_y = lambda j: (j * nz + z, rep)
    in_z1 = lambda j: (y * nz + zhalf * zq + j, rep)
    gram_1 = go(ny, y, in_y, lambda j: gram_y.at[y], lambda i: gram_y.at[i])

    hr = rank // 2
    slot = y * nz + zlow * 2 + zhalf
    piece = jnp.where(core == 0, pt[:hr], pt[hr:])
    lanes = 128
    tail = piece[:, lanes:]
    pt_all[core, slot, :hr] = piece[:, :lanes]
    pt_all[core, slot, hr:] = jnp.concatenate([tail[: hr // 2], tail[hr // 2 :]], axis=1)
    pt_1 = go(
        2, zhalf, lambda j: (y * nz + j * zq + zlow, rep),
        lambda j: pt_all.at[core, slot],
        lambda i: pt_all.at[core, y * nz + zlow * 2 + i],
    )

    wy = width // ny
    for i in range(ny):
        chunk = dot(pt, corr[:, i * wy : (i + 1) * wy], 1, 0, HI)
        m_part[:, i] = chunk.reshape(ng, r8, wy)
    m_1 = go(
        ng * ny, unit, at_unit, lambda j: m_part.at[j // ny, j % ny], lambda i: m_rs.at[i]
    )
    m_rs[unit] = m_part[g, y]

    gram_1.wait()
    gram_z[z] = total(gram_y, ny)
    gram_2 = go(
        nz, z, lambda j: (y * nz + j, rep), lambda j: gram_z.at[z], lambda i: gram_z.at[i]
    )
    pt_1.wait()
    pair = lambda i: pt_all.at[core, pl.ds(y * nz + i * 2, 2)]
    pt_2 = go(zq, zlow, in_z1, lambda j: pair(zlow), pair)

    m_1.wait()
    m_z1[zlow] = total(m_rs, ng * ny)
    m_3 = go(zq, zlow, in_z1, lambda j: m_z1.at[zlow], lambda i: m_z1.at[i])

    pt_2.wait()
    column = lambda i: pt_all.at[core, pl.ds(i * nz, nz)]
    pt_3 = go(ny, y, in_y, lambda j: column(y), column)
    gram_2.wait()
    gram_all[g] = total(gram_z, nz)
    gram_4 = go(ng, g, group, lambda j: gram_all.at[g], lambda i: gram_all.at[i])
    m_3.wait()
    w = h * 2 + zhalf
    m_z2[w] = total(m_z1, zq)
    m_4 = go(
        2 * nh, w, lambda j: (y * nz + j % 2 * zq + zlow, j // 2 * ng + g),
        lambda j: m_z2.at[w], lambda i: m_z2.at[i],
    )

    gram_4.wait()
    gram = gram_all[...].reshape(rank, rank)
    ri = lax.broadcasted_iota(jnp.int32, (rank, rank), 0)
    ci = lax.broadcasted_iota(jnp.int32, (rank, rank), 1)
    eye = (ri == ci).astype(F32)
    gram = gram + (0.0001 / rank) * jnp.sum(gram * eye) * eye
    full = jnp.concatenate([gram, eye], axis=1)
    x = [full[i : i + 8] for i in range(0, rank, 8)]
    sub = lax.broadcasted_iota(jnp.int32, (8, 1), 0)

    def eliminate(x, lo, hi):
        x = list(x)
        for j in range(lo, hi):
            b, i = divmod(j, 8)
            row = x[b][i : i + 1]
            scaled = row / row[:, j : j + 1]
            for k in range(b, len(x)):
                col = x[k][:, j : j + 1]
                if k == b:
                    col = jnp.where(sub > i, col, 0.0)
                x[k] = x[k] - col * scaled
        return x

    x = eliminate(x, 0, rank)
    m_4.wait()
    m_all[g, y] = total(m_z2, 2 * nh) * (1.0 / replicas)
    in_all = lambda i: m_all.at[i // ny, i % ny]
    m_6 = go(ng * ny, unit, at_unit, lambda j: m_all.at[g, y], in_all)
    pt_3.wait()
    side = lambda i: pt_all.at[i]
    pt_4 = go(2, core, lambda j: (outer, rep // 2 * 2 + j), lambda j: side(core), side)

    full = jnp.concatenate(x, axis=0)
    pivots = jnp.sum(full[:, :rank] * eye, axis=1, keepdims=True)
    inverse = full[:, rank:] * (1.0 / jnp.sqrt(pivots))
    hi, mid = parts(dot(p, inverse, 1, 1, HI))
    p_orth = jnp.concatenate([hi, hi, mid, mid], axis=1)
    for r in rounds[:-2]:
        r.drain()
    for k in (yp_copy, ym_copy):
        k(y, z, 0).wait_send()
    rp_copy(y_down, z, 0, half).wait_send()
    rm_copy(y_up, z, 0, half).wait_send()

    def drain(q):
        zb = place_of(q)
        yp_copy(y, zb, q).wait_send()
        ym_copy(y, zb, q).wait_send()
        rp_copy(y_down, zb, q).wait_send()
        rm_copy(y_up, zb, q).wait_send()
        to = z + 2 * (q % 2) - 1

        @pl.when(inside(to))
        def _():
            z_copy(zb, q + 2, to).wait_send()
            if ZROWS:
                zf_copy(zb, q + 2, to).wait_send()

    loop(1, last, drain)
    for q, to in ((1, z + 1), (2, z - 1)):

        @pl.when(inside(to))
        def _():
            z_copy(z, q, to).wait_send()
            if ZROWS:
                zf_copy(z, q, to).wait_send()

    pt_4.wait()

    def orthogonal(i, carry):
        yb, zb = i // (nz // 2), i % (nz // 2) * 2

        def block(zb):
            at = yb * nz + zb % zq * 2 + zb // zq
            head = jnp.concatenate([pt_all[0, at, :hr], pt_all[1, at, :hr]], axis=0)
            t0, t1 = pt_all[0, at, hr:], pt_all[1, at, hr:]
            w = rows - lanes
            tail = jnp.concatenate([t0[:, :w], t0[:, w:], t1[:, :w], t1[:, w:]], axis=0)
            return jnp.concatenate([head, tail], axis=1)

        two = jnp.concatenate([block(zb), block(zb + 1)], axis=1)
        hi, mid = parts(dot(inverse, two, 1, 0, HI))
        spread_src[i] = jnp.concatenate([hi, mid, hi, mid], axis=0)
        return carry

    lax.fori_loop(0, blocks // 2, orthogonal, 0, unroll=2)

    m_6.wait()
    for i in range(ny):
        cut = slice(i * wy, (i + 1) * wy)
        factor = dot(inverse, m_all[:, i].reshape(rank, wy), 1, 0, HI)
        factor_ref[:, cut] = factor
        hi, mid = parts(factor)
        factor = jnp.concatenate([hi, mid, hi, mid], axis=0)
        error_ref[:, cut] = corr[:, cut] - dot(p_orth, factor, 1, 0)
    columns = width // replicas
    both = factor_ref[:, pl.ds(pl.multiple_of(rep // 2 * (2 * columns), 2 * columns), 2 * columns)]
    hi, mid = parts(jnp.where(core == 0, both[:, :columns], both[:, columns:]))
    own = jnp.concatenate([hi, hi, mid, mid], axis=0)

    def spread(i, carry):
        update_ref[:, pl.ds(pl.multiple_of(i * 2 * rows, 2 * rows), 2 * rows)] = dot(
            own, spread_src[i], 0, 0
        ).astype(update_ref.dtype)
        return carry

    lax.fori_loop(0, blocks // 2, spread, 0, unroll=4)

    pt_4.drain()
    m_6.drain()


def body(ny, nz, nh, activations, out_grads, error_buffer, right_factor):
    replicas = lax.axis_size("rep")
    ng = replicas // nh
    blocks = ny * nz
    _, rows, depth = activations.shape
    _, tok, width = out_grads.shape
    rank = right_factor.shape[0]
    r8, wy, zq = rank // ng, width // ny, nz // 2
    dma = lambda n: pltpu.SemaphoreType.DMA((n,))
    vm = lambda *s: pltpu.VMEM(s, F32)
    update, new_error, new_factor = pl.pallas_call(
        functools.partial(kernel, ny, nz, nh, replicas),
        out_shape=(
            jax.ShapeDtypeStruct((width // replicas, blocks * rows), jnp.bfloat16),
            jax.ShapeDtypeStruct((rows, width), F32),
            jax.ShapeDtypeStruct((rank, width), F32),
        ),
        in_specs=[pl.BlockSpec(memory_space=pltpu.HBM)] * 4,
        out_specs=[pl.BlockSpec(memory_space=pltpu.VMEM)] * 3,
        scratch_shapes=[
            pltpu.VMEM((blocks, tok, width), jnp.bfloat16),
            pltpu.VMEM((rows, depth), jnp.bfloat16),
            vm(rank, width),
            vm(rows, width),
            vm(ng, rows // ng, rank),
            vm(ng, rows // ng, rank),
            vm(nh, rows // ng, rank),
            vm(ng, rows // ng, rank),
            vm(2, blocks, rank // 2 * rows // 128, 128),
            vm(ny, r8, rank),
            vm(nz, r8, rank),
            vm(ng, r8, rank),
            vm(ng, ny, r8, wy),
            vm(ng * ny, r8, wy),
            vm(zq, r8, wy),
            vm(2 * nh, r8, wy),
            vm(ng, ny, r8, wy),
            pltpu.VMEM((blocks // 2, 4 * rank, 2 * rows), jnp.bfloat16),
            dma(4),
        ]
        + [dma(2 * nz + 2)] * 12
        + [dma(112)] * 2,
        compiler_params=pltpu.CompilerParams(
            collective_id=0, has_side_effects=True, vmem_limit_bytes=63 * 2**20
        ),
    )(activations[0], out_grads[0], error_buffer[0], right_factor)
    return (update, new_error[None], new_factor)


def solution(mesh, ny=4, nh=2):
    nz = mesh.shape["outer"] // ny
    placed = (P("rep", "outer", None), P("rep", "outer", None), P("rep", "outer", None), P())
    return jax.shard_map(
        functools.partial(body, ny, nz, nh),
        mesh=mesh,
        in_specs=placed,
        out_specs=(P("rep", None), P("rep", "outer", None), P()),
        check_vma=False,
    )
```

```python
import functools

import jax
import jax.numpy as jnp
from jax import lax
from jax.experimental import pallas as pl
from jax.experimental.pallas import tpu as pltpu
from jax.sharding import PartitionSpec as P

ZROWS = 32
HI = lax.Precision.HIGHEST
F32 = jnp.float32


def dot(a, b, ca, cb, precision=None):
    return lax.dot_general(
        a, b, (((ca,), (cb,)), ((), ())), precision=precision, preferred_element_type=F32
    )


def copy_to(src, dst, send, recv, outer, rep):
    return pltpu.make_async_remote_copy(
        src_ref=src,
        dst_ref=dst,
        send_sem=send,
        recv_sem=recv,
        device_id={"outer": outer, "rep": rep},
        device_id_type=pl.DeviceIdType.MESH,
    )


def parts(x):
    hi = x.astype(jnp.bfloat16)
    return hi, (x - hi.astype(F32)).astype(jnp.bfloat16)


class Round:
    def __init__(self, n, me, place, src, dst, send, recv, first):
        def out(k):
            to = lax.rem(me + k, n)
            return copy_to(src(to), dst(me), send.at[first + k - 1], recv.at[first + k - 1], *place(to))

        def into(k):
            to, frm = lax.rem(me + k, n), lax.rem(me + n - k, n)
            return copy_to(src(to), dst(frm), send.at[first + k - 1], recv.at[first + k - 1], *place(to))

        self.n, self.out, self.into = n, out, into

    def each(self, act):
        if self.n <= 8:
            for k in range(1, self.n):
                act(k)
        else:
            lax.fori_loop(1, self.n, lambda k, carry: (act(k), carry)[1], 0)

    def start(self):
        self.each(lambda k: self.out(k).start())

    def wait(self):
        self.each(lambda k: self.into(k).wait_recv())

    def drain(self):
        self.each(lambda k: self.out(k).wait_send())


def kernel(
    ny, nz, nh, replicas,
    a_ref, g_ref, e_ref, r_ref,
    update_ref, error_ref, factor_ref,
    g_all, a_in, r_in, corr, p_part, p_rs, p_h, p_all8,
    pt_all, gram_y, gram_z, gram_all,
    m_part, m_rs, m_z1, m_z2, m_all, spread_src, load_sem,
    z_send, z_recv, zf_send, zf_recv, yp_send, yp_recv, ym_send, ym_recv,
    rp_send, rp_recv, rm_send, rm_recv, send, recv,
):
    ng = replicas // nh
    zq = nz // 2
    blocks = ny * nz
    tok, width = g_ref.shape
    rank = r_ref.shape[0]
    rows = a_ref.shape[0]
    outer, rep = lax.axis_index("outer"), lax.axis_index("rep")
    y, z = outer // nz, outer % nz
    h, g = rep // ng, rep % ng
    core = rep % 2
    zlow, zhalf = z % zq, z // zq
    y_up, y_down, y_far = (y + 1) % ny, (y + ny - 1) % ny, (y + 2) % ny
    h_other = (h + 1) % nh

    barrier = pltpu.get_barrier_semaphore()
    unit = g * ny + y
    at_unit = lambda j: (j % ny * nz + z, h * ng + j // ny)
    peers = [at_unit((unit + k) % (ng * ny)) for k in range(1, ng * ny)]
    peers += [(y * nz + (z + k) % nz, rep) for k in range(1, nz)]
    peers += [(outer, h_other * ng + g), (y * nz + (z + zq) % nz, h_other * ng + g)]
    for o, r in peers:
        pl.semaphore_signal(
            barrier, inc=1, device_id={"outer": o, "rep": r},
            device_id_type=pl.DeviceIdType.MESH,
        )
    loads = [
        pltpu.make_async_copy(src, dst, load_sem.at[i])
        for i, (src, dst) in enumerate(
            ((g_ref, g_all.at[outer]), (e_ref, corr), (a_ref, a_in), (r_ref, r_in))
        )
    ]
    for c in loads:
        c.start()
    loads[0].wait()
    pl.semaphore_wait(barrier, len(peers))

    half = tok // 2
    step_n = min(256, width)

    def multiply(block):
        a = a_in[:, pl.ds(pl.multiple_of(block * tok, tok), tok)]
        for n in range(0, width, step_n):
            corr[:, n : n + step_n] += dot(a, g_all[block, :, n : n + step_n], 1, 0)

    def place_of(q):
        d = (q + 1) // 2
        return z + d * (1 - 2 * (q % 2))

    def z_copy(zb, q, to):
        slot = g_all.at[y * nz + zb]
        return copy_to(slot, slot, z_send.at[q], z_recv.at[q], y * nz + to, rep)

    def yp_copy(yb, zb, q):
        slot = g_all.at[yb * nz + zb]
        return copy_to(slot, slot, yp_send.at[q], yp_recv.at[q], y_up * nz + z, rep)

    def ym_copy(yb, zb, q):
        slot = g_all.at[yb * nz + zb]
        return copy_to(slot, slot, ym_send.at[q], ym_recv.at[q], y_down * nz + z, rep)

    relayed = half - ZROWS // 2

    def rp_copy(yb, zb, q, n=relayed):
        slot = g_all.at[yb * nz + zb, pl.ds(0, n)]
        return copy_to(slot, slot, rp_send.at[q], rp_recv.at[q], y_up * nz + z, rep)

    def rm_copy(yb, zb, q, n=relayed):
        slot = g_all.at[yb * nz + zb, pl.ds(n, n)]
        return copy_to(slot, slot, rm_send.at[q], rm_recv.at[q], y_down * nz + z, rep)

    def zf_copy(zb, q, to):
        slot = g_all.at[y_far * nz + zb, pl.ds(tok - ZROWS, ZROWS)]
        return copy_to(slot, slot, zf_send.at[q], zf_recv.at[q], y * nz + to, rep)

    def inside(zb):
        return jnp.logical_and(zb >= 0, zb < nz)

    for q, to in ((1, z + 1), (2, z - 1)):

        @pl.when(inside(to))
        def _():
            z_copy(z, q, to).start()

    yp_copy(y, z, 0).start()
    ym_copy(y, z, 0).start()
    for c in loads[1:]:
        c.wait()
    multiply(outer)
    last = 2 * nz - 1

    def z_step(q, send_y=True):
        zb = place_of(q)

        @pl.when(inside(zb))
        def _():
            z_copy(zb, q, (z + 1) % nz).wait_recv()
            to = z + 2 * (q % 2) - 1

            @pl.when(inside(to))
            def _():
                z_copy(zb, q + 2, to).start()

            if send_y:
                z_sent(q)

    def z_sent(q):
        zb = place_of(q)
        yp_copy(y, zb, q).start()
        ym_copy(y, zb, q).start()
        multiply(y * nz + zb)

    def y_step(q, n):
        zb = place_of(q)
        yp_copy(y_down, zb, q).wait_recv()
        rp_copy(y_down, zb, q, n).start()
        ym_copy(y_up, zb, q).wait_recv()
        rm_copy(y_up, zb, q, n).start()

    def y_multiply(q):
        zb = place_of(q)
        multiply(y_down * nz + zb)
        multiply(y_up * nz + zb)

    def far_step(q, n):
        zb = place_of(q)
        rp_copy(y_far, zb, q, n).wait_recv()
        rm_copy(y_far, zb, q, n).wait_recv()
        multiply(y_far * nz + zb)

    def zf_step(q):
        zb = place_of(q)
        zf_copy(zb, q, (z + 1) % nz).wait_recv()
        to = z + 2 * (q % 2) - 1

        @pl.when(inside(to))
        def _():
            zf_copy(zb, q + 2, to).start()

    def loop(lo, hi, step):
        def guarded(q, carry):
            @pl.when(inside(place_of(q)))
            def _():
                step(q)

            return carry

        lax.fori_loop(lo, hi, guarded, 0)

    if ZROWS:
        loop(1, 3, z_step)
        y_step(0, half)
        y_multiply(0)
        loop(3, last, z_step)
        far_step(0, half)
        for q, to in ((1, z + 1), (2, z - 1)):

            @pl.when(inside(to))
            def _():
                zf_copy(z, q, to).start()

        def both(q):
            y_step(q, relayed)
            y_multiply(q)
            zf_step(q)

        loop(1, last, both)
    else:
        loop(1, last, z_step)
        y_step(0, half)
        y_multiply(0)

        def relay(q):
            y_step(q, relayed)
            y_multiply(q)

        loop(1, last, relay)
        far_step(0, half)
    loop(1, last, lambda q: far_step(q, relayed))

    rows8 = rows // ng
    part = dot(corr[...], r_in[...], 1, 1, HI) * (1.0 / replicas)
    p_part[...] = part.reshape(ng, rows8, rank)
    group = lambda j: (outer, h * ng + j)
    count = [0]

    def make(n, me, place, src, dst):
        first = count[0]
        count[0] += n - 1
        return Round(n, me, place, src, dst, send, recv, first)

    rounds = []

    def go(*args):
        r = make(*args)
        rounds.append(r)
        r.start()
        return r

    def total(ref, n):
        s = ref[0]
        for i in range(1, n):
            s = s + ref[i]
        return s

    rnd = go(ng, g, group, lambda j: p_part.at[j], lambda i: p_rs.at[i])
    p_rs[g] = p_part[g]
    rnd.wait()
    p_h[h] = total(p_rs, ng)
    if nh > 1:
        rnd = go(nh, h, lambda j: (outer, j * ng + g), lambda j: p_h.at[h], lambda i: p_h.at[i])
        rnd.wait()
    p_all8[g] = total(p_h, nh)
    rnd = go(ng, g, group, lambda j: p_all8.at[g], lambda i: p_all8.at[i])
    rnd.wait()
    p = p_all8[...].reshape(rows, rank)

    r8 = rank // ng
    pt = p.T
    gram_all[...] = dot(pt, pt, 1, 1, HI).reshape(ng, r8, rank)
    gram_y[y] = gram_all[g]
    in_y = lambda j: (j * nz + z, rep)
    in_z1 = lambda j: (y * nz + zhalf * zq + j, rep)
    gram_1 = go(ny, y, in_y, lambda j: gram_y.at[y], lambda i: gram_y.at[i])

    hr = rank // 2
    slot = y * nz + zlow * 2 + zhalf
    piece = jnp.where(core == 0, pt[:hr], pt[hr:])
    lanes = 128
    tail = piece[:, lanes:]
    pt_all[core, slot, :hr] = piece[:, :lanes]
    pt_all[core, slot, hr:] = jnp.concatenate([tail[: hr // 2], tail[hr // 2 :]], axis=1)
    pt_1 = go(
        2, zhalf, lambda j: (y * nz + j * zq + zlow, rep),
        lambda j: pt_all.at[core, slot],
        lambda i: pt_all.at[core, y * nz + zlow * 2 + i],
    )

    wy = width // ny
    for i in range(ny):
        chunk = dot(pt, corr[:, i * wy : (i + 1) * wy], 1, 0, HI)
        m_part[:, i] = chunk.reshape(ng, r8, wy)
    m_1 = go(
        ng * ny, unit, at_unit, lambda j: m_part.at[j // ny, j % ny], lambda i: m_rs.at[i]
    )
    m_rs[unit] = m_part[g, y]

    gram_1.wait()
    gram_z[z] = total(gram_y, ny)
    gram_2 = go(
        nz, z, lambda j: (y * nz + j, rep), lambda j: gram_z.at[z], lambda i: gram_z.at[i]
    )
    pt_1.wait()
    pair = lambda i: pt_all.at[core, pl.ds(y * nz + i * 2, 2)]
    pt_2 = go(zq, zlow, in_z1, lambda j: pair(zlow), pair)

    m_1.wait()
    m_z1[zlow] = total(m_rs, ng * ny)
    m_3 = go(zq, zlow, in_z1, lambda j: m_z1.at[zlow], lambda i: m_z1.at[i])

    pt_2.wait()
    column = lambda i: pt_all.at[core, pl.ds(i * nz, nz)]
    pt_3 = go(ny, y, in_y, lambda j: column(y), column)
    gram_2.wait()
    gram_all[g] = total(gram_z, nz)
    gram_4 = go(ng, g, group, lambda j: gram_all.at[g], lambda i: gram_all.at[i])
    m_3.wait()
    w = h * 2 + zhalf
    m_z2[w] = total(m_z1, zq)
    m_4 = go(
        2 * nh, w, lambda j: (y * nz + j % 2 * zq + zlow, j // 2 * ng + g),
        lambda j: m_z2.at[w], lambda i: m_z2.at[i],
    )

    gram_4.wait()
    gram = gram_all[...].reshape(rank, rank)
    ri = lax.broadcasted_iota(jnp.int32, (rank, rank), 0)
    ci = lax.broadcasted_iota(jnp.int32, (rank, rank), 1)
    eye = (ri == ci).astype(F32)
    gram = gram + (0.0001 / rank) * jnp.sum(gram * eye) * eye
    full = jnp.concatenate([gram, eye], axis=1)
    x = [full[i : i + 8] for i in range(0, rank, 8)]
    sub = lax.broadcasted_iota(jnp.int32, (8, 1), 0)

    def eliminate(x, lo, hi):
        x = list(x)
        for j in range(lo, hi):
            b, i = divmod(j, 8)
            row = x[b][i : i + 1]
            scaled = row / row[:, j : j + 1]
            for k in range(b, len(x)):
                col = x[k][:, j : j + 1]
                if k == b:
                    col = jnp.where(sub > i, col, 0.0)
                x[k] = x[k] - col * scaled
        return x

    most = rank * 5 // 8
    x = eliminate(x, 0, most)
    m_4.wait()
    m_all[g, y] = total(m_z2, 2 * nh) * (1.0 / replicas)
    in_all = lambda i: m_all.at[i // ny, i % ny]
    m_6 = go(ng * ny, unit, at_unit, lambda j: m_all.at[g, y], in_all)
    pt_3.wait()
    side = lambda i: pt_all.at[i]
    pt_4 = go(2, core, lambda j: (outer, rep // 2 * 2 + j), lambda j: side(core), side)

    x = eliminate(x, most, rank)
    full = jnp.concatenate(x, axis=0)
    pivots = jnp.sum(full[:, :rank] * eye, axis=1, keepdims=True)
    inverse = full[:, rank:] * (1.0 / jnp.sqrt(pivots))
    hi, mid = parts(dot(p, inverse, 1, 1, HI))
    p_orth = jnp.concatenate([hi, hi, mid, mid], axis=1)
    for r in rounds[:-2]:
        r.drain()
    for k in (yp_copy, ym_copy):
        k(y, z, 0).wait_send()
    rp_copy(y_down, z, 0, half).wait_send()
    rm_copy(y_up, z, 0, half).wait_send()

    def drain(q):
        zb = place_of(q)
        yp_copy(y, zb, q).wait_send()
        ym_copy(y, zb, q).wait_send()
        rp_copy(y_down, zb, q).wait_send()
        rm_copy(y_up, zb, q).wait_send()
        to = z + 2 * (q % 2) - 1

        @pl.when(inside(to))
        def _():
            z_copy(zb, q + 2, to).wait_send()
            if ZROWS:
                zf_copy(zb, q + 2, to).wait_send()

    loop(1, last, drain)
    for q, to in ((1, z + 1), (2, z - 1)):

        @pl.when(inside(to))
        def _():
            z_copy(z, q, to).wait_send()
            if ZROWS:
                zf_copy(z, q, to).wait_send()

    pt_4.wait()

    def orthogonal(i, carry):
        yb, zb = i // (nz // 2), i % (nz // 2) * 2

        def block(zb):
            at = yb * nz + zb % zq * 2 + zb // zq
            head = jnp.concatenate([pt_all[0, at, :hr], pt_all[1, at, :hr]], axis=0)
            t0, t1 = pt_all[0, at, hr:], pt_all[1, at, hr:]
            w = rows - lanes
            tail = jnp.concatenate([t0[:, :w], t0[:, w:], t1[:, :w], t1[:, w:]], axis=0)
            return jnp.concatenate([head, tail], axis=1)

        two = jnp.concatenate([block(zb), block(zb + 1)], axis=1)
        hi, mid = parts(dot(inverse, two, 1, 0, HI))
        spread_src[i] = jnp.concatenate([hi, mid, hi, mid], axis=0)
        return carry

    lax.fori_loop(0, blocks // 2, orthogonal, 0, unroll=2)

    m_6.wait()
    for i in range(ny):
        cut = slice(i * wy, (i + 1) * wy)
        factor = dot(inverse, m_all[:, i].reshape(rank, wy), 1, 0, HI)
        factor_ref[:, cut] = factor
        hi, mid = parts(factor)
        factor = jnp.concatenate([hi, mid, hi, mid], axis=0)
        error_ref[:, cut] = corr[:, cut] - dot(p_orth, factor, 1, 0)
    columns = width // replicas
    both = factor_ref[:, pl.ds(pl.multiple_of(rep // 2 * (2 * columns), 2 * columns), 2 * columns)]
    hi, mid = parts(jnp.where(core == 0, both[:, :columns], both[:, columns:]))
    own = jnp.concatenate([hi, hi, mid, mid], axis=0)

    def spread(i, carry):
        update_ref[:, pl.ds(pl.multiple_of(i * 2 * rows, 2 * rows), 2 * rows)] = dot(
            own, spread_src[i], 0, 0
        ).astype(update_ref.dtype)
        return carry

    lax.fori_loop(0, blocks // 2, spread, 0, unroll=4)

    pt_4.drain()
    m_6.drain()


def body(ny, nz, nh, activations, out_grads, error_buffer, right_factor):
    replicas = lax.axis_size("rep")
    ng = replicas // nh
    blocks = ny * nz
    _, rows, depth = activations.shape
    _, tok, width = out_grads.shape
    rank = right_factor.shape[0]
    r8, wy, zq = rank // ng, width // ny, nz // 2
    dma = lambda n: pltpu.SemaphoreType.DMA((n,))
    vm = lambda *s: pltpu.VMEM(s, F32)
    update, new_error, new_factor = pl.pallas_call(
        functools.partial(kernel, ny, nz, nh, replicas),
        out_shape=(
            jax.ShapeDtypeStruct((width // replicas, blocks * rows), jnp.bfloat16),
            jax.ShapeDtypeStruct((rows, width), F32),
            jax.ShapeDtypeStruct((rank, width), F32),
        ),
        in_specs=[pl.BlockSpec(memory_space=pltpu.HBM)] * 4,
        out_specs=[pl.BlockSpec(memory_space=pltpu.VMEM)] * 3,
        scratch_shapes=[
            pltpu.VMEM((blocks, tok, width), jnp.bfloat16),
            pltpu.VMEM((rows, depth), jnp.bfloat16),
            vm(rank, width),
            vm(rows, width),
            vm(ng, rows // ng, rank),
            vm(ng, rows // ng, rank),
            vm(nh, rows // ng, rank),
            vm(ng, rows // ng, rank),
            vm(2, blocks, rank // 2 * rows // 128, 128),
            vm(ny, r8, rank),
            vm(nz, r8, rank),
            vm(ng, r8, rank),
            vm(ng, ny, r8, wy),
            vm(ng * ny, r8, wy),
            vm(zq, r8, wy),
            vm(2 * nh, r8, wy),
            vm(ng, ny, r8, wy),
            pltpu.VMEM((blocks // 2, 4 * rank, 2 * rows), jnp.bfloat16),
            dma(4),
        ]
        + [dma(2 * nz + 2)] * 12
        + [dma(112)] * 2,
        compiler_params=pltpu.CompilerParams(
            collective_id=0, has_side_effects=True, vmem_limit_bytes=63 * 2**20
        ),
    )(activations[0], out_grads[0], error_buffer[0], right_factor)
    return (update, new_error[None], new_factor)


def solution(mesh, ny=4, nh=2):
    nz = mesh.shape["outer"] // ny
    placed = (P("rep", "outer", None), P("rep", "outer", None), P("rep", "outer", None), P())
    return jax.shard_map(
        functools.partial(body, ny, nz, nh),
        mesh=mesh,
        in_specs=placed,
        out_specs=(P("rep", None), P("rep", "outer", None), P()),
        check_vma=False,
    )
```
